256 devices in a mesh: rows: 64 (over z, y, core), batch: 4 (over x).
Axes of the slice: x: 4, y: 4, z: 8, core: 2. Of those that a mesh axis runs over, the one named last changes fastest.
Arguments:
- velocity: bfloat16 [8, 131072, 512], P(None, 'rows', 'batch'), may hold values from -48 to 48, as said below
Outputs:
- factor: float32 [8, 128, 128], replicated
- modes: float32 [8, 131072, 512], P(None, 'rows', 'batch')
The draws below stay inside these ranges and needn't reach their ends.
Inputs may be any that keep to these rules, and one draw needn't show every extreme that they name: velocity values of every plane, with nonzero spread in every window.
All inputs are finite; a program needn't handle non-finite values.
Results may differ from the reference program's by a relative error of at most 0.0003.
Values sent between devices are 32-bit elements; how exact they have to be, the bound alone decides.
No kernel may reach another device: no remote copies, remote signals or barrier semaphores. Data moves between devices by JAX's collectives and lax.ppermute only.
A program may use at most 128 MiB of HBM per device.

```python
import math
import jax
import jax.numpy as jnp
from jax import lax

PLANES = 8
WIN = 128
ROWS = 131072
WINDOWS = 4
SNAPS = 512
STACK = 524288


def draw_velocity(key, part):
    keys = jax.random.split(key, 3)
    shape = (PLANES, ROWS, SNAPS)
    rising = 0.5 + jnp.arange(ROWS, dtype=jnp.float32) / jnp.float32(ROWS)
    row_rough = jnp.exp(jax.random.uniform(keys[0], (PLANES, ROWS, 1), jnp.float32, math.log(0.3), math.log(3.0)))
    col_rough = jnp.exp(jax.random.uniform(keys[1], (PLANES, 1, SNAPS), jnp.float32, math.log(0.3), math.log(3.0)))
    base = jnp.clip(jax.random.normal(keys[2], shape, jnp.float32), -6.0, 6.0)
    values = base * row_rough * col_rough * rising[None, :, None]
    return jnp.clip(values, -48.0, 48.0).astype(jnp.bfloat16)


def setup_inputs(seed: int = 0) -> dict:
    seeds = jax.random.split(jax.random.key(seed), 2)
    velocity = draw_velocity(jax.random.fold_in(seeds[1], 71), 0)
    return {"velocity": velocity}


def one_plane(plane):
    blocks = plane.astype(jnp.float32).reshape(ROWS, WINDOWS, WIN)
    gram = jnp.einsum('rbk,rbj->kj', blocks, blocks, precision=lax.Precision.HIGHEST)
    lower = jnp.linalg.cholesky(gram / jnp.float32(STACK))
    factor = jnp.transpose(lower)
    identity = jnp.eye(WIN, dtype=jnp.float32)
    inverse = lax.linalg.triangular_solve(factor, identity, left_side=True, lower=False)
    modes = jnp.einsum('rbk,kj->rbj', blocks, inverse, precision=lax.Precision.HIGHEST)
    return (factor, modes.reshape(ROWS, SNAPS))

def reference(velocity):
    factor, modes = lax.map(one_plane, velocity)
    return (factor, modes)
```

```python
import jax
import jax.numpy as jnp
from jax import lax
from jax.experimental import pallas as pl
from jax.experimental.pallas import tpu as pltpu
from jax.sharding import PartitionSpec as P

BLOCK = 8
GROUP = 16
TILE = 512
LIMIT = 40 * 1024 * 1024


def packing(width):
    groups = width // GROUP
    half = groups // 2
    place = {}
    for a in range(half):
        for r in range(GROUP):
            place[a * GROUP + r] = (a * GROUP + r, 0)
            if a:
                place[(groups - a) * GROUP + r] = (a * GROUP + r, a * GROUP)
    for r in range(GROUP // 2):
        at = half * GROUP + r
        place[at] = (at, 0)
        place[at + GROUP // 2] = (at, width // 2)
    return place, half * GROUP + GROUP // 2


def gram_kernel(planes, width, v_ref, packed_ref, gram_ref):
    p = pl.program_id(0)
    v = v_ref[0]
    gram_ref[pl.ds(p, width, stride=planes), :] = lax.dot_general(
        v, v, (((0,), (0,)), ((), ())), preferred_element_type=jnp.float32
    )

    @pl.when(p == planes - 1)
    def _():
        place, _ = packing(width)
        lanes = lax.broadcasted_iota(jnp.int32, (planes, width), 1)
        for row, (at, roll) in place.items():
            if roll:
                continue
            value = gram_ref[row * planes : (row + 1) * planes, :]
            for other, (other_at, other_roll) in place.items():
                if other_at == at and other_roll:
                    moved = pltpu.roll(gram_ref[other * planes : (other + 1) * planes, :], other_roll, 1)
                    value = jnp.where(lanes < other_roll, moved, value)
            packed_ref[at * planes : (at + 1) * planes, :] = value


def lane(value, j):
    return jnp.broadcast_to(value[:, j : j + 1], value.shape)


def factor_rows(scale, packed_ref, u_ref, p_ref, width, planes):
    place, _ = packing(width)
    lanes = lax.broadcasted_iota(jnp.int32, (planes, width), 1)

    def given(i):
        at, roll = place[i]
        row = packed_ref[at * planes : (at + 1) * planes, :]
        return (pltpu.roll(row, width - roll, 1) if roll else row) * scale

    for start in range(0, width, BLOCK):
        inside = (lanes >= start) & (lanes < start + BLOCK)
        rows = [jnp.where(lanes >= start, given(start + i), 0.0) for i in range(BLOCK)]

        def older(k, rows):
            rows = list(rows)
            at = pl.ds(pl.multiple_of(k * planes, planes), planes)
            source = p_ref[at, :]
            for i in range(BLOCK):
                rows[i] = rows[i] - lane(source, start + i) * source
            p_ref[at, :] = jnp.where(inside, 0.0, source)
            return tuple(rows)

        if start:
            rows = list(lax.fori_loop(0, start, older, tuple(rows), unroll=8))
        cell = {(i, j): lane(rows[i], start + j) for i in range(BLOCK) for j in range(i, BLOCK)}
        for k in range(BLOCK):
            pivot = cell[k, k]
            root = lax.rsqrt(pivot)
            root = root * (1.5 - 0.5 * pivot * root * root)
            for j in range(k + 1, BLOCK):
                cell[k, j] = cell[k, j] * root
            for i in range(k + 1, BLOCK):
                for j in range(i, BLOCK):
                    cell[i, j] = cell[i, j] - cell[k, i] * cell[k, j]
            here = lanes == start + k
            whole = rows[k] * root
            u_ref[pl.ds(start + k, planes, stride=width), :] = jnp.where(lanes >= start + k, whole, 0.0)
            whole = jnp.where(here, root, whole)
            p_ref[(start + k) * planes : (start + k + 1) * planes, :] = jnp.where(
                (lanes <= start + k) | (lanes >= start + BLOCK), whole, 0.0
            )
            for i in range(k + 1, BLOCK):
                rows[i] = jnp.where(here, 0.0, rows[i]) - cell[k, i] * whole


def modes_kernel(scale, planes, width, packed_ref, v_hbm, u_ref, m_hbm, p_ref, v_ref, m_ref, in_sem, out_sem):
    def fetch(p):
        return pltpu.make_async_copy(v_hbm.at[p], v_ref.at[p], in_sem.at[p])

    def put(p):
        return pltpu.make_async_copy(m_ref.at[p], m_hbm.at[p], out_sem.at[p])

    for p in range(planes):
        fetch(p).start()
    factor_rows(scale, packed_ref, u_ref, p_ref, width, planes)
    rows_dev = v_ref.shape[1]
    for p in range(planes):
        rest = p_ref[pl.ds(p, width, stride=planes), :]
        high = rest.astype(jnp.bfloat16)
        rest = rest - high.astype(jnp.float32)
        middle = rest.astype(jnp.bfloat16)
        low = (rest - middle.astype(jnp.float32)).astype(jnp.bfloat16)
        weights = jnp.concatenate(
            [
                jnp.concatenate([high, middle], axis=1),
                jnp.concatenate([low, jnp.zeros_like(low)], axis=1),
            ],
            axis=0,
        )
        fetch(p).wait()

        def tile(t, _):
            at = pl.ds(pl.multiple_of(t * TILE, TILE), TILE)
            v = v_ref[p, at, :]
            both = lax.dot_general(
                jnp.concatenate([v, v], axis=1),
                weights,
                (((1,), (1,)), ((), ())),
                preferred_element_type=jnp.float32,
            )
            m_ref[p, at, :] = both[:, :width] + both[:, width:]
            return 0

        lax.fori_loop(0, rows_dev // TILE, tile, 0)
        put(p).start()
    for p in range(planes):
        put(p).wait()


def index(z, y, core):
    return (z * 4 + y) * 2 + core


def rows_perm(move):
    return [(index(z, y, c), index(*move(z, y, c))) for z in range(8) for y in range(4) for c in range(2)]


def total(x):
    core = lax.axis_index("rows") % 2
    here = lax.axis_index("batch")
    other_core = rows_perm(lambda z, y, c: (z, y, 1 - c))
    n = x.shape[0] // 2
    x = lax.dynamic_slice_in_dim(x, core * n, n, 0) + lax.ppermute(
        lax.dynamic_slice_in_dim(x, (1 - core) * n, n, 0), "rows", other_core
    )
    m = n // 4
    shift = {d: [(i, (i + d) % 4) for i in range(4)] for d in (1, 2, 3)}
    got = [
        lax.ppermute(lax.dynamic_slice_in_dim(x, ((here + d) % 4) * m, m, 0), "batch", shift[d]) for d in (1, 2, 3)
    ]
    x = lax.dynamic_slice_in_dim(x, here * m, m, 0) + got[0] + got[1] + got[2]
    got = [lax.ppermute(x, "rows", rows_perm(lambda z, y, c: (z, (y + d) % 4, c))) for d in (1, 2, 3)]
    x = (x + got[1]) + (got[0] + got[2])
    for bit in (1, 2, 4):
        x = x + lax.ppermute(x, "rows", rows_perm(lambda z, y, c: (z ^ bit, y, c)))
    got = [x] + [lax.ppermute(x, "batch", shift[d]) for d in (1, 2, 3)]
    x = jnp.concatenate(
        [
            jnp.where(
                here == j,
                got[0],
                jnp.where(here == (j + 1) % 4, got[1], jnp.where(here == (j + 2) % 4, got[2], got[3])),
            )
            for j in range(4)
        ],
        axis=0,
    )
    y = lax.ppermute(x, "rows", other_core)
    return jnp.concatenate([jnp.where(core == 0, x, y), jnp.where(core == 0, y, x)], axis=0)


def shards(velocity):
    planes, rows_dev, width = velocity.shape
    stack = rows_dev * lax.axis_size("rows") * lax.axis_size("batch")
    _, packed_rows = packing(width)
    packed = pl.pallas_call(
        lambda *refs: gram_kernel(planes, width, *refs),
        grid=(planes,),
        in_specs=[pl.BlockSpec((1, rows_dev, width), lambda p: (p, 0, 0))],
        out_specs=pl.BlockSpec((packed_rows * planes, width), lambda p: (0, 0)),
        out_shape=jax.ShapeDtypeStruct((packed_rows * planes, width), jnp.float32),
        scratch_shapes=[pltpu.VMEM((width * planes, width), jnp.float32)],
        compiler_params=pltpu.CompilerParams(vmem_limit_bytes=LIMIT),
        name="gram",
    )(velocity)
    packed = total(packed)
    factor, modes = pl.pallas_call(
        lambda *refs: modes_kernel(1.0 / stack, planes, width, *refs),
        in_specs=[pl.BlockSpec(memory_space=pltpu.VMEM), pl.BlockSpec(memory_space=pl.ANY)],
        out_specs=[pl.BlockSpec(memory_space=pltpu.VMEM), pl.BlockSpec(memory_space=pl.ANY)],
        out_shape=[
            jax.ShapeDtypeStruct((planes * width, width), jnp.float32),
            jax.ShapeDtypeStruct((planes, rows_dev, width), jnp.float32),
        ],
        scratch_shapes=[
            pltpu.VMEM((width * planes, width), jnp.float32),
            pltpu.VMEM((planes, rows_dev, width), jnp.bfloat16),
            pltpu.VMEM((planes, rows_dev, width), jnp.float32),
            pltpu.SemaphoreType.DMA((planes,)),
            pltpu.SemaphoreType.DMA((planes,)),
        ],
        compiler_params=pltpu.CompilerParams(vmem_limit_bytes=LIMIT),
        name="factor_modes",
    )(packed, velocity)
    return (factor.reshape(planes, width, width), modes)


def solution(mesh):
    placed = (P(None, "rows", "batch"),)
    return jax.shard_map(
        shards,
        mesh=mesh,
        in_specs=placed,
        out_specs=(P(), P(None, "rows", "batch")),
        check_vma=False,
    )
```

```python
import jax
import jax.numpy as jnp
from jax import lax
from jax.experimental import pallas as pl
from jax.experimental.pallas import tpu as pltpu
from jax.sharding import PartitionSpec as P

BLOCK = 8
PANEL = 16
GROUP = 16
LIMIT = 58 * 1024 * 1024


def packing(width):
    groups = width // GROUP
    half = groups // 2
    place = {}
    for a in range(half):
        for r in range(GROUP):
            place[a * GROUP + r] = (a * GROUP + r, 0)
            if a:
                place[(groups - a) * GROUP + r] = (a * GROUP + r, a * GROUP)
    for r in range(GROUP // 2):
        at = half * GROUP + r
        place[at] = (at, 0)
        place[at + GROUP // 2] = (at, width // 2)
    return place, half * GROUP + GROUP // 2


def gram_kernel(planes, width, v_hbm, packed_ref, gram_ref, v_ref, sem):
    def fetch(p):
        return pltpu.make_async_copy(v_hbm.at[p], v_ref.at[p], sem.at[p])

    for p in range(planes):
        fetch(p).start()
    for p in range(planes):
        fetch(p).wait()
        v = v_ref[p]
        gram_ref[pl.ds(p, width, stride=planes), :] = lax.dot_general(
            v, v, (((0,), (0,)), ((), ())), preferred_element_type=jnp.float32
        )
    place, _ = packing(width)
    lanes = lax.broadcasted_iota(jnp.int32, (planes, width), 1)
    for row, (at, roll) in place.items():
        if roll:
            continue
        value = gram_ref[row * planes : (row + 1) * planes, :]
        for other, (other_at, other_roll) in place.items():
            if other_at == at and other_roll:
                moved = pltpu.roll(gram_ref[other * planes : (other + 1) * planes, :], other_roll, 1)
                value = jnp.where(lanes < other_roll, moved, value)
        packed_ref[at * planes : (at + 1) * planes, :] = value


def lane(value, j):
    return jnp.broadcast_to(value[:, j : j + 1], value.shape)


def parts(value):
    high = value.astype(jnp.bfloat16)
    value = value - high.astype(jnp.float32)
    middle = value.astype(jnp.bfloat16)
    return high, middle, (value - middle.astype(jnp.float32)).astype(jnp.bfloat16)


def factor_rows(scale, packed_ref, u_ref, p_ref, x_ref, width, planes):
    place, _ = packing(width)
    lanes = lax.broadcasted_iota(jnp.int32, (planes, width), 1)
    wide = lax.broadcasted_iota(jnp.int32, (width, width), 1)

    def row(ref, i):
        return ref[i * planes : (i + 1) * planes, :]

    for i, (at, roll) in place.items():
        value = row(packed_ref, at)
        x_ref[i * planes : (i + 1) * planes, :] = (pltpu.roll(value, width - roll, 1) if roll else value) * scale

    for first in range(0, width, PANEL):
        last = first + PANEL
        for start in range(first, last, BLOCK):
            kept = (lanes < first) | (lanes >= start)
            inside = (lanes >= start) & (lanes < start + BLOCK)
            rows = [jnp.where(kept, row(x_ref, start + i), 0.0) for i in range(BLOCK)]
            for k in range(first, start):
                source = row(p_ref, k)
                for i in range(BLOCK):
                    rows[i] = rows[i] - lane(source, start + i) * source
                p_ref[k * planes : (k + 1) * planes, :] = jnp.where(inside, 0.0, source)
            cell = {(i, j): lane(rows[i], start + j) for i in range(BLOCK) for j in range(i, BLOCK)}
            for k in range(BLOCK):
                pivot = cell[k, k]
                root = lax.rsqrt(pivot)
                root = root * (1.5 - 0.5 * pivot * root * root)
                for j in range(k + 1, BLOCK):
                    cell[k, j] = cell[k, j] * root
                for i in range(k + 1, BLOCK):
                    for j in range(i, BLOCK):
                        cell[i, j] = cell[i, j] - cell[k, i] * cell[k, j]
                here = lanes == start + k
                whole = rows[k] * root
                u_ref[pl.ds(start + k, planes, stride=width), :] = jnp.where(lanes >= start + k, whole, 0.0)
                whole = jnp.where(here, root, whole)
                p_ref[(start + k) * planes : (start + k + 1) * planes, :] = jnp.where(
                    (lanes <= start + k) | (lanes >= start + BLOCK), whole, 0.0
                )
                for i in range(k + 1, BLOCK):
                    rows[i] = jnp.where(here, 0.0, rows[i]) - cell[k, i] * whole
        if last == width:
            break
        done = (wide[last:, :] >= first) & (wide[last:, :] < last)
        for p in range(planes):
            high, middle, low = parts(p_ref[pl.ds(first * planes + p, PANEL, stride=planes), :])
            change = lax.dot_general(
                jnp.concatenate([high, high, middle, high, low, middle], axis=0),
                jnp.concatenate([high, middle, high, low, high, middle], axis=0),
                (((0,), (0,)), ((), ())),
                preferred_element_type=jnp.float32,
            )
            at = pl.ds(last * planes + p, width - last, stride=planes)
            x_ref[at, :] = jnp.where(done, 0.0, x_ref[at, :]) - change[last:, :]


def modes_kernel(
    scale, planes, width, packed_ref, v_hbm, u_hbm, m_hbm, u_ref, p_ref, x_ref, v_ref, m_ref, in_sem, out_sem, u_sem
):
    def fetch(p):
        return pltpu.make_async_copy(v_hbm.at[p], v_ref.at[p], in_sem.at[p])

    def put(p):
        return pltpu.make_async_copy(m_ref.at[p], m_hbm.at[p], out_sem.at[p])

    for p in range(planes):
        fetch(p).start()
    factor_rows(scale, packed_ref, u_ref, p_ref, x_ref, width, planes)
    put_factor = pltpu.make_async_copy(u_ref, u_hbm, u_sem)
    put_factor.start()
    low_half = lax.broadcasted_iota(jnp.int32, (width, width), 0) >= lax.broadcasted_iota(
        jnp.int32, (width, width), 1
    )
    for p in range(planes):
        high, middle, low = parts(jnp.where(low_half, p_ref[pl.ds(p, width, stride=planes), :], 0.0))
        weights = jnp.concatenate(
            [
                jnp.concatenate([high, middle], axis=1),
                jnp.concatenate([low, jnp.zeros_like(low)], axis=1),
            ],
            axis=0,
        )
        fetch(p).wait()
        v = v_ref[p]
        both = lax.dot_general(
            jnp.concatenate([v, v], axis=1),
            weights,
            (((1,), (1,)), ((), ())),
            preferred_element_type=jnp.float32,
        )
        m_ref[p] = both[:, :width] + both[:, width:]
        put(p).start()
    put_factor.wait()
    for p in range(planes):
        put(p).wait()


def index(z, y, core):
    return (z * 4 + y) * 2 + core


def rows_perm(move):
    return [(index(z, y, c), index(*move(z, y, c))) for z in range(8) for y in range(4) for c in range(2)]


def total(x):
    core = lax.axis_index("rows") % 2
    here = lax.axis_index("batch")
    other_core = rows_perm(lambda z, y, c: (z, y, 1 - c))
    n = x.shape[0] // 2
    x = lax.dynamic_slice_in_dim(x, core * n, n, 0) + lax.ppermute(
        lax.dynamic_slice_in_dim(x, (1 - core) * n, n, 0), "rows", other_core
    )
    m = n // 4
    shift = {d: [(i, (i + d) % 4) for i in range(4)] for d in (1, 2, 3)}
    got = [
        lax.ppermute(lax.dynamic_slice_in_dim(x, ((here + d) % 4) * m, m, 0), "batch", shift[d]) for d in (1, 2, 3)
    ]
    x = lax.dynamic_slice_in_dim(x, here * m, m, 0) + got[0] + got[1] + got[2]
    got = [lax.ppermute(x, "rows", rows_perm(lambda z, y, c: (z, (y + d) % 4, c))) for d in (1, 2, 3)]
    x = (x + got[1]) + (got[0] + got[2])
    for bit in (1, 2, 4):
        x = x + lax.ppermute(x, "rows", rows_perm(lambda z, y, c: (z ^ bit, y, c)))
    got = [x] + [lax.ppermute(x, "batch", shift[d]) for d in (1, 2, 3)]
    x = jnp.concatenate(
        [
            jnp.where(
                here == j,
                got[0],
                jnp.where(here == (j + 1) % 4, got[1], jnp.where(here == (j + 2) % 4, got[2], got[3])),
            )
            for j in range(4)
        ],
        axis=0,
    )
    y = lax.ppermute(x, "rows", other_core)
    return jnp.concatenate([jnp.where(core == 0, x, y), jnp.where(core == 0, y, x)], axis=0)


def shards(velocity):
    planes, rows_dev, width = velocity.shape
    stack = rows_dev * lax.axis_size("rows") * lax.axis_size("batch")
    _, packed_rows = packing(width)
    hbm = pl.BlockSpec(memory_space=pltpu.HBM)
    vmem = pl.BlockSpec(memory_space=pltpu.VMEM)
    packed = pl.pallas_call(
        lambda *refs: gram_kernel(planes, width, *refs),
        in_specs=[hbm],
        out_specs=vmem,
        out_shape=jax.ShapeDtypeStruct((packed_rows * planes, width), jnp.float32),
        scratch_shapes=[
            pltpu.VMEM((width * planes, width), jnp.float32),
            pltpu.VMEM((planes, rows_dev, width), jnp.bfloat16),
            pltpu.SemaphoreType.DMA((planes,)),
        ],
        compiler_params=pltpu.CompilerParams(vmem_limit_bytes=LIMIT),
        name="gram",
    )(velocity)
    packed = total(packed)
    factor, modes = pl.pallas_call(
        lambda *refs: modes_kernel(1.0 / stack, planes, width, *refs),
        in_specs=[vmem, hbm],
        out_specs=[hbm, hbm],
        out_shape=[
            jax.ShapeDtypeStruct((planes * width, width), jnp.float32),
            jax.ShapeDtypeStruct((planes, rows_dev, width), jnp.float32),
        ],
        scratch_shapes=[
            pltpu.VMEM((planes * width, width), jnp.float32),
            pltpu.VMEM((width * planes, width), jnp.float32),
            pltpu.VMEM((width * planes, width), jnp.float32),
            pltpu.VMEM((planes, rows_dev, width), jnp.bfloat16),
            pltpu.VMEM((planes, rows_dev, width), jnp.float32),
            pltpu.SemaphoreType.DMA((planes,)),
            pltpu.SemaphoreType.DMA((planes,)),
            pltpu.SemaphoreType.DMA,
        ],
        compiler_params=pltpu.CompilerParams(vmem_limit_bytes=LIMIT),
        name="factor_modes",
    )(packed, velocity)
    return (factor.reshape(planes, width, width), modes)


def solution(mesh):
    placed = (P(None, "rows", "batch"),)
    return jax.shard_map(
        shards,
        mesh=mesh,
        in_specs=placed,
        out_specs=(P(), P(None, "rows", "batch")),
        check_vma=False,
    )
```

```python
import jax
import jax.numpy as jnp
from jax import lax
from jax.experimental import pallas as pl
from jax.experimental.pallas import tpu as pltpu
from jax.sharding import PartitionSpec as P

BLOCK = 8
PANEL = 16
GROUP = 16
LIMIT = 51 * 1024 * 1024


def packing(width):
    groups = width // GROUP
    half = groups // 2
    place = {}
    for a in range(half):
        for r in range(GROUP):
            place[a * GROUP + r] = (a * GROUP + r, 0)
            if a:
                place[(groups - a) * GROUP + r] = (a * GROUP + r, a * GROUP)
    for r in range(GROUP // 2):
        at = half * GROUP + r
        place[at] = (at, 0)
        place[at + GROUP // 2] = (at, width // 2)
    return place, half * GROUP + GROUP // 2


def gram_kernel(planes, width, v_hbm, packed_ref, gram_ref, v_ref, sem):
    def fetch(p):
        return pltpu.make_async_copy(v_hbm.at[p], v_ref.at[p], sem.at[p])

    for p in range(planes):
        fetch(p).start()
    for p in range(planes):
        fetch(p).wait()
        v = v_ref[p]
        gram_ref[pl.ds(p, width, stride=planes), :] = lax.dot_general(
            v, v, (((0,), (0,)), ((), ())), preferred_element_type=jnp.float32
        )
    place, _ = packing(width)
    lanes = lax.broadcasted_iota(jnp.int32, (planes, width), 1)
    for row, (at, roll) in place.items():
        if roll:
            continue
        value = gram_ref[row * planes : (row + 1) * planes, :]
        for other, (other_at, other_roll) in place.items():
            if other_at == at and other_roll:
                moved = pltpu.roll(gram_ref[other * planes : (other + 1) * planes, :], other_roll, 1)
                value = jnp.where(lanes < other_roll, moved, value)
        packed_ref[at * planes : (at + 1) * planes, :] = value


def lane(value, j):
    return jnp.broadcast_to(value[:, j : j + 1], value.shape)


def parts(value):
    high = value.astype(jnp.bfloat16)
    value = value - high.astype(jnp.float32)
    middle = value.astype(jnp.bfloat16)
    return high, middle, (value - middle.astype(jnp.float32)).astype(jnp.bfloat16)


def factor_rows(scale, packed_ref, u_ref, p_ref, x_ref, width, planes):
    place, _ = packing(width)
    lanes = lax.broadcasted_iota(jnp.int32, (planes, width), 1)
    wide = lax.broadcasted_iota(jnp.int32, (width, width), 1)

    def row(ref, i):
        return ref[i * planes : (i + 1) * planes, :]

    for i, (at, roll) in place.items():
        value = row(packed_ref, at)
        x_ref[i * planes : (i + 1) * planes, :] = (pltpu.roll(value, width - roll, 1) if roll else value) * scale

    for first in range(0, width, PANEL):
        last = first + PANEL
        for start in range(first, last, BLOCK):
            kept = (lanes < first) | (lanes >= start)
            inside = (lanes >= start) & (lanes < start + BLOCK)
            rows = [jnp.where(kept, row(x_ref, start + i), 0.0) for i in range(BLOCK)]
            for k in range(first, start):
                source = row(p_ref, k)
                for i in range(BLOCK):
                    rows[i] = rows[i] - lane(source, start + i) * source
                p_ref[k * planes : (k + 1) * planes, :] = jnp.where(inside, 0.0, source)
            cell = {(i, j): lane(rows[i], start + j) for i in range(BLOCK) for j in range(i, BLOCK)}
            for k in range(BLOCK):
                pivot = cell[k, k]
                root = lax.rsqrt(pivot)
                root = root * (1.5 - 0.5 * pivot * root * root)
                for j in range(k + 1, BLOCK):
                    cell[k, j] = cell[k, j] * root
                for i in range(k + 1, BLOCK):
                    for j in range(i, BLOCK):
                        cell[i, j] = cell[i, j] - cell[k, i] * cell[k, j]
                here = lanes == start + k
                whole = rows[k] * root
                u_ref[pl.ds(start + k, planes, stride=width), :] = jnp.where(lanes >= start + k, whole, 0.0)
                whole = jnp.where(here, root, whole)
                p_ref[(start + k) * planes : (start + k + 1) * planes, :] = jnp.where(
                    (lanes <= start + k) | (lanes >= start + BLOCK), whole, 0.0
                )
                for i in range(k + 1, BLOCK):
                    rows[i] = jnp.where(here, 0.0, rows[i]) - cell[k, i] * whole
        if last == width:
            break
        done = (wide[last:, :] >= first) & (wide[last:, :] < last)
        for p in range(planes):
            high, middle, low = parts(p_ref[pl.ds(first * planes + p, PANEL, stride=planes), :])
            change = lax.dot_general(
                jnp.concatenate([high, high, middle, high, low, middle], axis=0),
                jnp.concatenate([high, middle, high, low, high, middle], axis=0),
                (((0,), (0,)), ((), ())),
                preferred_element_type=jnp.float32,
            )
            at = pl.ds(last * planes + p, width - last, stride=planes)
            x_ref[at, :] = jnp.where(done, 0.0, x_ref[at, :]) - change[last:, :]


def modes_kernel(
    scale, planes, width, packed_ref, v_hbm, u_hbm, m_hbm, u_ref, p_ref, x_ref, v_ref, m_ref, in_sem, out_sem, u_sem
):
    def fetch(p):
        return pltpu.make_async_copy(v_hbm.at[p], v_ref.at[p], in_sem.at[p])

    def put(p):
        return pltpu.make_async_copy(m_ref.at[p], m_hbm.at[p], out_sem.at[p])

    for p in range(planes):
        fetch(p).start()
    factor_rows(scale, packed_ref, u_ref, p_ref, x_ref, width, planes)
    put_factor = pltpu.make_async_copy(u_ref, u_hbm, u_sem)
    put_factor.start()
    low_half = lax.broadcasted_iota(jnp.int32, (width, width), 0) >= lax.broadcasted_iota(
        jnp.int32, (width, width), 1
    )
    for p in range(planes):
        high, middle, low = parts(jnp.where(low_half, p_ref[pl.ds(p, width, stride=planes), :], 0.0))
        weights = jnp.concatenate(
            [
                jnp.concatenate([high, middle], axis=1),
                jnp.concatenate([low, jnp.zeros_like(low)], axis=1),
            ],
            axis=0,
        )
        fetch(p).wait()
        v = v_ref[p]
        both = lax.dot_general(
            jnp.concatenate([v, v], axis=1),
            weights,
            (((1,), (1,)), ((), ())),
            preferred_element_type=jnp.float32,
        )
        m_ref[p] = both[:, :width] + both[:, width:]
        put(p).start()
    put_factor.wait()
    for p in range(planes):
        put(p).wait()


def flip(x, axis, mask):
    step = {"z": 8, "y": 2, "core": 1}
    if axis == "x":
        return lax.ppermute(x, "batch", [(i, i ^ mask) for i in range(lax.axis_size("batch"))])
    return lax.ppermute(x, "rows", [(i, i ^ (mask * step[axis])) for i in range(lax.axis_size("rows"))])


def total(x):
    core = lax.axis_index("rows") % 2
    here = lax.axis_index("batch")
    half = x.shape[0] // 2
    x = lax.dynamic_slice_in_dim(x, core * half, half, 0) + flip(
        lax.dynamic_slice_in_dim(x, (1 - core) * half, half, 0), "core", 1
    )
    part = half // 4
    got = [flip(lax.dynamic_slice_in_dim(x, (here ^ d) * part, part, 0), "x", d) for d in (1, 2, 3)]
    x = (lax.dynamic_slice_in_dim(x, here * part, part, 0) + got[1]) + (got[0] + got[2])
    x = x + flip(x, "y", 1)
    x = x + flip(x, "y", 3)
    x = x + flip(x, "z", 7)
    got = [flip(x, "z", d) for d in (1, 2, 3)]
    x = (x + got[1]) + (got[0] + got[2])
    got = [x] + [flip(x, "x", d) for d in (1, 2, 3)]
    x = jnp.concatenate(
        [
            jnp.where(here == j, got[0], jnp.where(here == j ^ 1, got[1], jnp.where(here == j ^ 2, got[2], got[3])))
            for j in range(4)
        ],
        axis=0,
    )
    y = flip(x, "core", 1)
    return jnp.concatenate([jnp.where(core == 0, x, y), jnp.where(core == 0, y, x)], axis=0)


def shards(velocity):
    planes, rows_dev, width = velocity.shape
    stack = rows_dev * lax.axis_size("rows") * lax.axis_size("batch")
    _, packed_rows = packing(width)
    hbm = pl.BlockSpec(memory_space=pltpu.HBM)
    vmem = pl.BlockSpec(memory_space=pltpu.VMEM)
    packed = pl.pallas_call(
        lambda *refs: gram_kernel(planes, width, *refs),
        in_specs=[hbm],
        out_specs=vmem,
        out_shape=jax.ShapeDtypeStruct((packed_rows * planes, width), jnp.float32),
        scratch_shapes=[
            pltpu.VMEM((width * planes, width), jnp.float32),
            pltpu.VMEM((planes, rows_dev, width), jnp.bfloat16),
            pltpu.SemaphoreType.DMA((planes,)),
        ],
        compiler_params=pltpu.CompilerParams(vmem_limit_bytes=LIMIT),
        name="gram",
    )(velocity)
    packed = total(packed)
    factor, modes = pl.pallas_call(
        lambda *refs: modes_kernel(1.0 / stack, planes, width, *refs),
        in_specs=[vmem, hbm],
        out_specs=[hbm, hbm],
        out_shape=[
            jax.ShapeDtypeStruct((planes * width, width), jnp.float32),
            jax.ShapeDtypeStruct((planes, rows_dev, width), jnp.float32),
        ],
        scratch_shapes=[
            pltpu.VMEM((planes * width, width), jnp.float32),
            pltpu.VMEM((width * planes, width), jnp.float32),
            pltpu.VMEM((width * planes, width), jnp.float32),
            pltpu.VMEM((planes, rows_dev, width), jnp.bfloat16),
            pltpu.VMEM((planes, rows_dev, width), jnp.float32),
            pltpu.SemaphoreType.DMA((planes,)),
            pltpu.SemaphoreType.DMA((planes,)),
            pltpu.SemaphoreType.DMA,
        ],
        compiler_params=pltpu.CompilerParams(vmem_limit_bytes=LIMIT),
        name="factor_modes",
    )(packed, velocity)
    return (factor.reshape(planes, width, width), modes)


def solution(mesh):
    placed = (P(None, "rows", "batch"),)
    return jax.shard_map(
        shards,
        mesh=mesh,
        in_specs=placed,
        out_specs=(P(), P(None, "rows", "batch")),
        check_vma=False,
    )
```

```python
import jax
import jax.numpy as jnp
from jax import lax
from jax.experimental import pallas as pl
from jax.experimental.pallas import tpu as pltpu
from jax.sharding import PartitionSpec as P

BLOCK = 8
PANEL = 16
GROUP = 16
LIMIT = 51 * 1024 * 1024


def packing(width):
    groups = width // GROUP
    half = groups // 2
    place = {}
    for a in range(half):
        for r in range(GROUP):
            place[a * GROUP + r] = (a * GROUP + r, 0)
            if a:
                place[(groups - a) * GROUP + r] = (a * GROUP + r, a * GROUP)
    for r in range(GROUP // 2):
        at = half * GROUP + r
        place[at] = (at, 0)
        place[at + GROUP // 2] = (at, width // 2)
    return place, half * GROUP + GROUP // 2


def gram_kernel(planes, width, v_hbm, packed_ref, gram_ref, v_ref, sem):
    def fetch(p):
        return pltpu.make_async_copy(v_hbm.at[p], v_ref.at[p], sem.at[p])

    for p in range(planes):
        fetch(p).start()
    for p in range(planes):
        fetch(p).wait()
        v = v_ref[p]
        gram_ref[pl.ds(p, width, stride=planes), :] = lax.dot_general(
            v, v, (((0,), (0,)), ((), ())), preferred_element_type=jnp.float32
        )
    place, _ = packing(width)
    lanes = lax.broadcasted_iota(jnp.int32, (planes, width), 1)
    for row, (at, roll) in place.items():
        if roll:
            continue
        value = gram_ref[row * planes : (row + 1) * planes, :]
        for other, (other_at, other_roll) in place.items():
            if other_at == at and other_roll:
                moved = pltpu.roll(gram_ref[other * planes : (other + 1) * planes, :], other_roll, 1)
                value = jnp.where(lanes < other_roll, moved, value)
        packed_ref[at * planes : (at + 1) * planes, :] = value


def lane(value, j):
    return jnp.broadcast_to(value[:, j : j + 1], value.shape)


def parts(value):
    high = value.astype(jnp.bfloat16)
    value = value - high.astype(jnp.float32)
    middle = value.astype(jnp.bfloat16)
    return high, middle, (value - middle.astype(jnp.float32)).astype(jnp.bfloat16)


def factor_rows(scale, packed_ref, u_ref, p_ref, x_ref, width, planes):
    place, _ = packing(width)
    lanes = lax.broadcasted_iota(jnp.int32, (planes, width), 1)
    wide = lax.broadcasted_iota(jnp.int32, (width, width), 1)

    def row(ref, i):
        return ref[i * planes : (i + 1) * planes, :]

    for i, (at, roll) in place.items():
        value = row(packed_ref, at)
        x_ref[i * planes : (i + 1) * planes, :] = (pltpu.roll(value, width - roll, 1) if roll else value) * scale

    for first in range(0, width, PANEL):
        last = first + PANEL
        for start in range(first, last, BLOCK):
            kept = (lanes < first) | (lanes >= start)
            inside = (lanes >= start) & (lanes < start + BLOCK)
            rows = [jnp.where(kept, row(x_ref, start + i), 0.0) for i in range(BLOCK)]
            for k in range(first, start):
                source = row(p_ref, k)
                for i in range(BLOCK):
                    rows[i] = rows[i] - lane(source, start + i) * source
                p_ref[k * planes : (k + 1) * planes, :] = jnp.where(inside, 0.0, source)
            cell = {(i, j): lane(rows[i], start + j) for i in range(BLOCK) for j in range(i, BLOCK)}
            for k in range(BLOCK):
                pivot = cell[k, k]
                root = lax.rsqrt(pivot)
                root = root * (1.5 - 0.5 * pivot * root * root)
                for j in range(k + 1, BLOCK):
                    cell[k, j] = cell[k, j] * root
                for i in range(k + 1, BLOCK):
                    for j in range(i, BLOCK):
                        cell[i, j] = cell[i, j] - cell[k, i] * cell[k, j]
                here = lanes == start + k
                whole = rows[k] * root
                u_ref[pl.ds(start + k, planes, stride=width), :] = jnp.where(lanes >= start + k, whole, 0.0)
                whole = jnp.where(here, root, whole)
                p_ref[(start + k) * planes : (start + k + 1) * planes, :] = jnp.where(
                    (lanes <= start + k) | (lanes >= start + BLOCK), whole, 0.0
                )
                for i in range(k + 1, BLOCK):
                    rows[i] = jnp.where(here, 0.0, rows[i]) - cell[k, i] * whole
        if last == width:
            break
        done = (wide[last:, :] >= first) & (wide[last:, :] < last)
        for p in range(planes):
            high, middle, low = parts(p_ref[pl.ds(first * planes + p, PANEL, stride=planes), :])
            change = lax.dot_general(
                jnp.concatenate([high, high, middle, high, low, middle], axis=0),
                jnp.concatenate([high, middle, high, low, high, middle], axis=0),
                (((0,), (0,)), ((), ())),
                preferred_element_type=jnp.float32,
            )
            at = pl.ds(last * planes + p, width - last, stride=planes)
            x_ref[at, :] = jnp.where(done, 0.0, x_ref[at, :]) - change[last:, :]


def modes_kernel(
    scale, planes, width, packed_ref, v_hbm, u_hbm, m_hbm, u_ref, p_ref, x_ref, v_ref, m_ref, in_sem, out_sem, u_sem
):
    def fetch(p):
        return pltpu.make_async_copy(v_hbm.at[p], v_ref.at[p], in_sem.at[p])

    def put(p):
        return pltpu.make_async_copy(m_ref.at[p], m_hbm.at[p], out_sem.at[p])

    for p in range(planes):
        fetch(p).start()
    factor_rows(scale, packed_ref, u_ref, p_ref, x_ref, width, planes)
    put_factor = pltpu.make_async_copy(u_ref, u_hbm, u_sem)
    put_factor.start()
    low_half = lax.broadcasted_iota(jnp.int32, (width, width), 0) >= lax.broadcasted_iota(
        jnp.int32, (width, width), 1
    )
    for p in range(planes):
        high, middle, low = parts(jnp.where(low_half, p_ref[pl.ds(p, width, stride=planes), :], 0.0))
        weights = jnp.concatenate(
            [
                jnp.concatenate([high, middle], axis=1),
                jnp.concatenate([low, jnp.zeros_like(low)], axis=1),
            ],
            axis=0,
        )
        fetch(p).wait()
        v = v_ref[p]
        both = lax.dot_general(
            jnp.concatenate([v, v], axis=1),
            weights,
            (((1,), (1,)), ((), ())),
            preferred_element_type=jnp.float32,
        )
        m_ref[p] = both[:, :width] + both[:, width:]
        put(p).start()
    put_factor.wait()
    for p in range(planes):
        put(p).wait()


def flip(x, axis, mask):
    step = {"z": 8, "y": 2}
    width = lax.axis_size("batch")
    pairs = []
    for row in range(lax.axis_size("rows")):
        for col in range(width):
            to_row, to_col = (row, col ^ mask) if axis == "x" else (row ^ (mask * step[axis]), col)
            pairs.append((row * width + col, (to_row ^ (mask & 1)) * width + to_col))
    return lax.ppermute(x, ("rows", "batch"), pairs)


def other_core(x):
    return lax.ppermute(x, "rows", [(i, i ^ 1) for i in range(lax.axis_size("rows"))])


def total(x):
    row, here = lax.axis_index("rows"), lax.axis_index("batch")
    role = (row ^ (row // 2) ^ (row // 8) ^ here) % 2
    half = x.shape[0] // 2
    x = lax.dynamic_slice_in_dim(x, role * half, half, 0) + other_core(
        lax.dynamic_slice_in_dim(x, (1 - role) * half, half, 0)
    )
    part = half // 4
    got = [flip(lax.dynamic_slice_in_dim(x, (here ^ d) * part, part, 0), "x", d) for d in (1, 2, 3)]
    x = (lax.dynamic_slice_in_dim(x, here * part, part, 0) + got[1]) + (got[0] + got[2])
    got = [flip(x, "y", d) for d in (1, 2, 3)]
    x = (x + got[1]) + (got[0] + got[2])
    x = x + flip(x, "z", 7)
    got = [flip(x, "z", d) for d in (1, 2, 3)]
    x = (x + got[1]) + (got[0] + got[2])
    got = [x] + [flip(x, "x", d) for d in (1, 2, 3)]
    x = jnp.concatenate(
        [
            jnp.where(here == j, got[0], jnp.where(here == j ^ 1, got[1], jnp.where(here == j ^ 2, got[2], got[3])))
            for j in range(4)
        ],
        axis=0,
    )
    y = other_core(x)
    return jnp.concatenate([jnp.where(role == 0, x, y), jnp.where(role == 0, y, x)], axis=0)


def shards(velocity):
    planes, rows_dev, width = velocity.shape
    stack = rows_dev * lax.axis_size("rows") * lax.axis_size("batch")
    _, packed_rows = packing(width)
    hbm = pl.BlockSpec(memory_space=pltpu.HBM)
    vmem = pl.BlockSpec(memory_space=pltpu.VMEM)
    packed = pl.pallas_call(
        lambda *refs: gram_kernel(planes, width, *refs),
        in_specs=[hbm],
        out_specs=vmem,
        out_shape=jax.ShapeDtypeStruct((packed_rows * planes, width), jnp.float32),
        scratch_shapes=[
            pltpu.VMEM((width * planes, width), jnp.float32),
            pltpu.VMEM((planes, rows_dev, width), jnp.bfloat16),
            pltpu.SemaphoreType.DMA((planes,)),
        ],
        compiler_params=pltpu.CompilerParams(vmem_limit_bytes=LIMIT),
        name="gram",
    )(velocity)
    packed = total(packed)
    factor, modes = pl.pallas_call(
        lambda *refs: modes_kernel(1.0 / stack, planes, width, *refs),
        in_specs=[vmem, hbm],
        out_specs=[hbm, hbm],
        out_shape=[
            jax.ShapeDtypeStruct((planes * width, width), jnp.float32),
            jax.ShapeDtypeStruct((planes, rows_dev, width), jnp.float32),
        ],
        scratch_shapes=[
            pltpu.VMEM((planes * width, width), jnp.float32),
            pltpu.VMEM((width * planes, width), jnp.float32),
            pltpu.VMEM((width * planes, width), jnp.float32),
            pltpu.VMEM((planes, rows_dev, width), jnp.bfloat16),
            pltpu.VMEM((planes, rows_dev, width), jnp.float32),
            pltpu.SemaphoreType.DMA((planes,)),
            pltpu.SemaphoreType.DMA((planes,)),
            pltpu.SemaphoreType.DMA,
        ],
        compiler_params=pltpu.CompilerParams(vmem_limit_bytes=LIMIT),
        name="factor_modes",
    )(packed, velocity)
    return (factor.reshape(planes, width, width), modes)


def solution(mesh):
    placed = (P(None, "rows", "batch"),)
    return jax.shard_map(
        shards,
        mesh=mesh,
        in_specs=placed,
        out_specs=(P(), P(None, "rows", "batch")),
        check_vma=False,
    )
```

```python
import jax
import jax.numpy as jnp
from jax import lax
from jax.experimental import pallas as pl
from jax.experimental.pallas import tpu as pltpu
from jax.sharding import PartitionSpec as P

BLOCK = 8
PANEL = 2 * BLOCK
GROUP = 16
TILE = 256
LIMIT = 51 * 1024 * 1024


def packing(width):
    groups = width // GROUP
    half = groups // 2
    place = {}
    for a in range(half):
        for r in range(GROUP):
            place[a * GROUP + r] = (a * GROUP + r, 0)
            if a:
                place[(groups - a) * GROUP + r] = (a * GROUP + r, a * GROUP)
    for r in range(GROUP // 2):
        at = half * GROUP + r
        place[at] = (at, 0)
        place[at + GROUP // 2] = (at, width // 2)
    return place, half * GROUP + GROUP // 2


def gram_kernel(planes, width, v_hbm, packed_ref, gram_ref, v_ref, sem):
    def fetch(p):
        return pltpu.make_async_copy(v_hbm.at[p], v_ref.at[p], sem.at[p])

    for p in range(planes):
        fetch(p).start()
    for p in range(planes):
        fetch(p).wait()
        v = v_ref[p]
        gram_ref[pl.ds(p, width, stride=planes), :] = lax.dot_general(
            v, v, (((0,), (0,)), ((), ())), preferred_element_type=jnp.float32
        )
    place, _ = packing(width)
    lanes = lax.broadcasted_iota(jnp.int32, (planes, width), 1)
    for row, (at, roll) in place.items():
        if roll:
            continue
        value = gram_ref[row * planes : (row + 1) * planes, :]
        for other, (other_at, other_roll) in place.items():
            if other_at == at and other_roll:
                moved = pltpu.roll(gram_ref[other * planes : (other + 1) * planes, :], other_roll, 1)
                value = jnp.where(lanes < other_roll, moved, value)
        packed_ref[at * planes : (at + 1) * planes, :] = value


def lane(value, j):
    return jnp.broadcast_to(value[:, j : j + 1], value.shape)


def parts(value):
    high = value.astype(jnp.bfloat16)
    value = value - high.astype(jnp.float32)
    middle = value.astype(jnp.bfloat16)
    return high, middle, (value - middle.astype(jnp.float32)).astype(jnp.bfloat16)


def factor_rows(scale, packed_ref, u_ref, p_ref, x_ref, width, planes):
    place, _ = packing(width)
    lanes = lax.broadcasted_iota(jnp.int32, (planes, width), 1)
    wide = lax.broadcasted_iota(jnp.int32, (width, width), 1)

    def row(ref, i):
        return ref[i * planes : (i + 1) * planes, :]

    for i, (at, roll) in place.items():
        value = row(packed_ref, at)
        x_ref[i * planes : (i + 1) * planes, :] = (pltpu.roll(value, width - roll, 1) if roll else value) * scale

    for first in range(0, width, PANEL):
        last = first + PANEL
        for start in (first, first + BLOCK):
            kept = (lanes < first) | (lanes >= start)
            rows = [jnp.where(kept, row(x_ref, start + i), 0.0) for i in range(BLOCK)]
            if start > first:
                inside = (lanes >= start) & (lanes < start + BLOCK)
                for k in range(BLOCK):
                    for i in range(BLOCK):
                        rows[i] = rows[i] - cell[k, BLOCK + i] * older[k]
                    p_ref[(first + k) * planes : (first + k + 1) * planes, :] = jnp.where(inside, 0.0, older[k])
            columns = last - start
            cell = {(i, j): lane(rows[i], start + j) for i in range(BLOCK) for j in range(i, columns)}
            older = []
            for k in range(BLOCK):
                root = lax.rsqrt(cell[k, k])
                for j in range(k + 1, columns):
                    cell[k, j] = cell[k, j] * root
                for i in range(k + 1, BLOCK):
                    for j in range(i, columns):
                        cell[i, j] = cell[i, j] - cell[k, i] * cell[k, j]
                here = lanes == start + k
                whole = rows[k] * root
                u_ref[pl.ds(start + k, planes, stride=width), :] = jnp.where(lanes >= start + k, whole, 0.0)
                whole = jnp.where(here, root, whole)
                older.append(jnp.where((lanes <= start + k) | (lanes >= start + BLOCK), whole, 0.0))
                for i in range(k + 1, BLOCK):
                    rows[i] = jnp.where(here, 0.0, rows[i]) - cell[k, i] * whole
            if start > first:
                for k in range(BLOCK):
                    p_ref[(start + k) * planes : (start + k + 1) * planes, :] = older[k]
        if last == width:
            break
        done = (wide[last:, :] >= first) & (wide[last:, :] < last)
        for p in range(planes):
            high, middle, low = parts(p_ref[pl.ds(first * planes + p, PANEL, stride=planes), :])
            change = lax.dot_general(
                jnp.concatenate([high, high, middle, high, low, middle], axis=0),
                jnp.concatenate([high, middle, high, low, high, middle], axis=0),
                (((0,), (0,)), ((), ())),
                preferred_element_type=jnp.float32,
            )
            at = pl.ds(last * planes + p, width - last, stride=planes)
            x_ref[at, :] = jnp.where(done, 0.0, x_ref[at, :]) - change[last:, :]


def modes_kernel(
    scale, planes, width, packed_ref, v_hbm, u_hbm, m_hbm, u_ref, p_ref, x_ref, v_ref, m_ref, in_sem, out_sem, u_sem
):
    def fetch(p):
        return pltpu.make_async_copy(v_hbm.at[p], v_ref.at[p], in_sem.at[p])

    tiles = v_ref.shape[1] // TILE

    def put(p, t):
        at = pl.ds(t * TILE, TILE)
        return pltpu.make_async_copy(m_ref.at[p, at], m_hbm.at[p, at], out_sem.at[p * tiles + t])

    for p in range(planes):
        fetch(p).start()
    factor_rows(scale, packed_ref, u_ref, p_ref, x_ref, width, planes)
    put_factor = pltpu.make_async_copy(u_ref, u_hbm, u_sem)
    put_factor.start()
    low_half = lax.broadcasted_iota(jnp.int32, (width, width), 0) >= lax.broadcasted_iota(
        jnp.int32, (width, width), 1
    )
    for p in range(planes):
        high, middle, low = parts(jnp.where(low_half, p_ref[pl.ds(p, width, stride=planes), :], 0.0))
        weights = jnp.concatenate(
            [
                jnp.concatenate([high, middle], axis=1),
                jnp.concatenate([low, jnp.zeros_like(low)], axis=1),
            ],
            axis=0,
        )
        fetch(p).wait()
        for t in range(tiles):
            v = v_ref[p, t * TILE : (t + 1) * TILE, :]
            both = lax.dot_general(
                jnp.concatenate([v, v], axis=1),
                weights,
                (((1,), (1,)), ((), ())),
                preferred_element_type=jnp.float32,
            )
            m_ref[p, t * TILE : (t + 1) * TILE, :] = both[:, :width] + both[:, width:]
            put(p, t).start()
    put_factor.wait()
    for p in range(planes):
        for t in range(tiles):
            put(p, t).wait()


def flip(x, axis, mask):
    step = {"z": 8, "y": 2}
    width = lax.axis_size("batch")
    pairs = []
    for row in range(lax.axis_size("rows")):
        for col in range(width):
            to_row, to_col = (row, col ^ mask) if axis == "x" else (row ^ (mask * step[axis]), col)
            pairs.append((row * width + col, (to_row ^ (mask & 1)) * width + to_col))
    return lax.ppermute(x, ("rows", "batch"), pairs)


def other_core(x):
    return lax.ppermute(x, "rows", [(i, i ^ 1) for i in range(lax.axis_size("rows"))])


def total(x):
    row, here = lax.axis_index("rows"), lax.axis_index("batch")
    role = (row ^ (row // 2) ^ (row // 8) ^ here) % 2
    half = x.shape[0] // 2
    x = lax.dynamic_slice_in_dim(x, role * half, half, 0) + other_core(
        lax.dynamic_slice_in_dim(x, (1 - role) * half, half, 0)
    )
    part = half // 4
    got = [flip(lax.dynamic_slice_in_dim(x, (here ^ d) * part, part, 0), "x", d) for d in (1, 2, 3)]
    x = (lax.dynamic_slice_in_dim(x, here * part, part, 0) + got[1]) + (got[0] + got[2])
    got = [flip(x, "y", d) for d in (1, 2, 3)]
    x = (x + got[1]) + (got[0] + got[2])
    x = x + flip(x, "z", 7)
    got = [flip(x, "z", d) for d in (1, 2, 3)]
    x = (x + got[1]) + (got[0] + got[2])
    got = [x] + [flip(x, "x", d) for d in (1, 2, 3)]
    x = jnp.concatenate(
        [
            jnp.where(here == j, got[0], jnp.where(here == j ^ 1, got[1], jnp.where(here == j ^ 2, got[2], got[3])))
            for j in range(4)
        ],
        axis=0,
    )
    y = other_core(x)
    return jnp.concatenate([jnp.where(role == 0, x, y), jnp.where(role == 0, y, x)], axis=0)


def shards(velocity):
    planes, rows_dev, width = velocity.shape
    stack = rows_dev * lax.axis_size("rows") * lax.axis_size("batch")
    _, packed_rows = packing(width)
    hbm = pl.BlockSpec(memory_space=pltpu.HBM)
    vmem = pl.BlockSpec(memory_space=pltpu.VMEM)
    packed = pl.pallas_call(
        lambda *refs: gram_kernel(planes, width, *refs),
        in_specs=[hbm],
        out_specs=vmem,
        out_shape=jax.ShapeDtypeStruct((packed_rows * planes, width), jnp.float32),
        scratch_shapes=[
            pltpu.VMEM((width * planes, width), jnp.float32),
            pltpu.VMEM((planes, rows_dev, width), jnp.bfloat16),
            pltpu.SemaphoreType.DMA((planes,)),
        ],
        compiler_params=pltpu.CompilerParams(vmem_limit_bytes=LIMIT),
        name="gram",
    )(velocity)
    packed = total(packed)
    factor, modes = pl.pallas_call(
        lambda *refs: modes_kernel(1.0 / stack, planes, width, *refs),
        in_specs=[vmem, hbm],
        out_specs=[hbm, hbm],
        out_shape=[
            jax.ShapeDtypeStruct((planes * width, width), jnp.float32),
            jax.ShapeDtypeStruct((planes, rows_dev, width), jnp.float32),
        ],
        scratch_shapes=[
            pltpu.VMEM((planes * width, width), jnp.float32),
            pltpu.VMEM((width * planes, width), jnp.float32),
            pltpu.VMEM((width * planes, width), jnp.float32),
            pltpu.VMEM((planes, rows_dev, width), jnp.bfloat16),
            pltpu.VMEM((planes, rows_dev, width), jnp.float32),
            pltpu.SemaphoreType.DMA((planes,)),
            pltpu.SemaphoreType.DMA((planes * (rows_dev // TILE),)),
            pltpu.SemaphoreType.DMA,
        ],
        compiler_params=pltpu.CompilerParams(vmem_limit_bytes=LIMIT),
        name="factor_modes",
    )(packed, velocity)
    return (factor.reshape(planes, width, width), modes)


def solution(mesh):
    placed = (P(None, "rows", "batch"),)
    return jax.shard_map(
        shards,
        mesh=mesh,
        in_specs=placed,
        out_specs=(P(), P(None, "rows", "batch")),
        check_vma=False,
    )
```

```python
import jax
import jax.numpy as jnp
from jax import lax
from jax.experimental import pallas as pl
from jax.experimental.pallas import tpu as pltpu
from jax.sharding import PartitionSpec as P

BLOCK = 8
PANEL = 2 * BLOCK
GROUP = 16
TILE = 512
LIMIT = 51 * 1024 * 1024


def packing(width):
    groups = width // GROUP
    half = groups // 2
    place = {}
    for a in range(half):
        for r in range(GROUP):
            place[a * GROUP + r] = (a * GROUP + r, 0)
            if a:
                place[(groups - a) * GROUP + r] = (a * GROUP + r, a * GROUP)
    for r in range(GROUP // 2):
        at = half * GROUP + r
        place[at] = (at, 0)
        place[at + GROUP // 2] = (at, width // 2)
    return place, half * GROUP + GROUP // 2


def gram_kernel(planes, width, v_hbm, packed_ref, gram_ref, v_ref, sem):
    def fetch(p):
        return pltpu.make_async_copy(v_hbm.at[p], v_ref.at[p], sem.at[p])

    for p in range(planes):
        fetch(p).start()
    for p in range(planes):
        fetch(p).wait()
        v = v_ref[p]
        gram_ref[pl.ds(p, width, stride=planes), :] = lax.dot_general(
            v, v, (((0,), (0,)), ((), ())), preferred_element_type=jnp.float32
        )
    place, _ = packing(width)
    lanes = lax.broadcasted_iota(jnp.int32, (planes, width), 1)
    for row, (at, roll) in place.items():
        if roll:
            continue
        value = gram_ref[row * planes : (row + 1) * planes, :]
        for other, (other_at, other_roll) in place.items():
            if other_at == at and other_roll:
                moved = pltpu.roll(gram_ref[other * planes : (other + 1) * planes, :], other_roll, 1)
                value = jnp.where(lanes < other_roll, moved, value)
        packed_ref[at * planes : (at + 1) * planes, :] = value


def lane(value, j):
    return jnp.broadcast_to(value[:, j : j + 1], value.shape)


def parts(value):
    high = value.astype(jnp.bfloat16)
    value = value - high.astype(jnp.float32)
    middle = value.astype(jnp.bfloat16)
    return high, middle, (value - middle.astype(jnp.float32)).astype(jnp.bfloat16)


def factor_rows(scale, packed_ref, u_ref, p_ref, x_ref, width, planes):
    place, _ = packing(width)
    lanes = lax.broadcasted_iota(jnp.int32, (planes, width), 1)
    wide = lax.broadcasted_iota(jnp.int32, (width, width), 1)

    def row(ref, i):
        return ref[i * planes : (i + 1) * planes, :]

    for i, (at, roll) in place.items():
        value = row(packed_ref, at)
        x_ref[i * planes : (i + 1) * planes, :] = (pltpu.roll(value, width - roll, 1) if roll else value) * scale

    for first in range(0, width, PANEL):
        last = first + PANEL
        for start in (first, first + BLOCK):
            kept = (lanes < first) | (lanes >= start)
            rows = [jnp.where(kept, row(x_ref, start + i), 0.0) for i in range(BLOCK)]
            if start > first:
                inside = (lanes >= start) & (lanes < start + BLOCK)
                for k in range(BLOCK):
                    for i in range(BLOCK):
                        rows[i] = rows[i] - cell[k, BLOCK + i] * older[k]
                    p_ref[(first + k) * planes : (first + k + 1) * planes, :] = jnp.where(inside, 0.0, older[k])
            columns = last - start
            cell = {(i, j): lane(rows[i], start + j) for i in range(BLOCK) for j in range(i, columns)}
            older = []
            for k in range(BLOCK):
                root = lax.rsqrt(cell[k, k])
                for j in range(k + 1, columns):
                    cell[k, j] = cell[k, j] * root
                for i in range(k + 1, BLOCK):
                    for j in range(i, columns):
                        cell[i, j] = cell[i, j] - cell[k, i] * cell[k, j]
                here = lanes == start + k
                whole = rows[k] * root
                u_ref[pl.ds(start + k, planes, stride=width), :] = jnp.where(lanes >= start + k, whole, 0.0)
                whole = jnp.where(here, root, whole)
                older.append(jnp.where((lanes <= start + k) | (lanes >= start + BLOCK), whole, 0.0))
                for i in range(k + 1, BLOCK):
                    rows[i] = jnp.where(here, 0.0, rows[i]) - cell[k, i] * whole
            if start > first:
                for k in range(BLOCK):
                    p_ref[(start + k) * planes : (start + k + 1) * planes, :] = older[k]
        if last == width:
            break
        done = (wide[last:, :] >= first) & (wide[last:, :] < last)
        for p in range(planes):
            high, middle, low = parts(p_ref[pl.ds(first * planes + p, PANEL, stride=planes), :])
            change = lax.dot_general(
                jnp.concatenate([high, high, middle, high, low, middle], axis=0),
                jnp.concatenate([high, middle, high, low, high, middle], axis=0),
                (((0,), (0,)), ((), ())),
                preferred_element_type=jnp.float32,
            )
            at = pl.ds(last * planes + p, width - last, stride=planes)
            x_ref[at, :] = jnp.where(done, 0.0, x_ref[at, :]) - change[last:, :]


def modes_kernel(
    scale, planes, width, packed_ref, v_hbm, u_hbm, m_hbm, u_ref, p_ref, x_ref, v_ref, m_ref, in_sem, out_sem, u_sem
):
    def fetch(p):
        return pltpu.make_async_copy(v_hbm.at[p], v_ref.at[p], in_sem.at[p])

    tiles = v_ref.shape[1] // TILE

    def put(p, t):
        at = pl.ds(t * TILE, TILE)
        return pltpu.make_async_copy(m_ref.at[p, at], m_hbm.at[p, at], out_sem.at[p * tiles + t])

    for p in range(planes):
        fetch(p).start()
    factor_rows(scale, packed_ref, u_ref, p_ref, x_ref, width, planes)
    put_factor = pltpu.make_async_copy(u_ref, u_hbm, u_sem)
    put_factor.start()
    low_half = lax.broadcasted_iota(jnp.int32, (width, width), 0) >= lax.broadcasted_iota(
        jnp.int32, (width, width), 1
    )
    for p in range(planes):
        high, middle, low = parts(jnp.where(low_half, p_ref[pl.ds(p, width, stride=planes), :], 0.0))
        weights = jnp.concatenate(
            [
                jnp.concatenate([high, middle], axis=1),
                jnp.concatenate([low, jnp.zeros_like(low)], axis=1),
            ],
            axis=0,
        )
        fetch(p).wait()
        for t in range(tiles):
            v = v_ref[p, t * TILE : (t + 1) * TILE, :]
            both = lax.dot_general(
                jnp.concatenate([v, v], axis=1),
                weights,
                (((1,), (1,)), ((), ())),
                preferred_element_type=jnp.float32,
            )
            m_ref[p, t * TILE : (t + 1) * TILE, :] = both[:, :width] + both[:, width:]
            put(p, t).start()
    put_factor.wait()
    for p in range(planes):
        for t in range(tiles):
            put(p, t).wait()


def flip(x, axis, mask):
    step = {"z": 8, "y": 2}
    width = lax.axis_size("batch")
    pairs = []
    for row in range(lax.axis_size("rows")):
        for col in range(width):
            to_row, to_col = (row, col ^ mask) if axis == "x" else (row ^ (mask * step[axis]), col)
            pairs.append((row * width + col, (to_row ^ (mask & 1)) * width + to_col))
    return lax.ppermute(x, ("rows", "batch"), pairs)


def other_core(x):
    return lax.ppermute(x, "rows", [(i, i ^ 1) for i in range(lax.axis_size("rows"))])


def total(x):
    row, here = lax.axis_index("rows"), lax.axis_index("batch")
    role = (row ^ (row // 2) ^ (row // 8) ^ here) % 2
    half = x.shape[0] // 2
    x = lax.dynamic_slice_in_dim(x, role * half, half, 0) + other_core(
        lax.dynamic_slice_in_dim(x, (1 - role) * half, half, 0)
    )
    part = half // 4
    got = [flip(lax.dynamic_slice_in_dim(x, (here ^ d) * part, part, 0), "x", d) for d in (1, 2, 3)]
    x = (lax.dynamic_slice_in_dim(x, here * part, part, 0) + got[1]) + (got[0] + got[2])
    got = [flip(x, "y", d) for d in (1, 2, 3)]
    x = (x + got[1]) + (got[0] + got[2])
    x = x + flip(x, "z", 7)
    got = [flip(x, "z", d) for d in (1, 2, 3)]
    x = (x + got[1]) + (got[0] + got[2])
    got = [x] + [flip(x, "x", d) for d in (1, 2, 3)]
    x = jnp.concatenate(
        [
            jnp.where(here == j, got[0], jnp.where(here == j ^ 1, got[1], jnp.where(here == j ^ 2, got[2], got[3])))
            for j in range(4)
        ],
        axis=0,
    )
    y = other_core(x)
    return jnp.concatenate([jnp.where(role == 0, x, y), jnp.where(role == 0, y, x)], axis=0)


def shards(velocity):
    planes, rows_dev, width = velocity.shape
    stack = rows_dev * lax.axis_size("rows") * lax.axis_size("batch")
    _, packed_rows = packing(width)
    hbm = pl.BlockSpec(memory_space=pltpu.HBM)
    vmem = pl.BlockSpec(memory_space=pltpu.VMEM)
    packed = pl.pallas_call(
        lambda *refs: gram_kernel(planes, width, *refs),
        in_specs=[hbm],
        out_specs=vmem,
        out_shape=jax.ShapeDtypeStruct((packed_rows * planes, width), jnp.float32),
        scratch_shapes=[
            pltpu.VMEM((width * planes, width), jnp.float32),
            pltpu.VMEM((planes, rows_dev, width), jnp.bfloat16),
            pltpu.SemaphoreType.DMA((planes,)),
        ],
        compiler_params=pltpu.CompilerParams(vmem_limit_bytes=LIMIT),
        name="gram",
    )(velocity)
    packed = total(packed)
    factor, modes = pl.pallas_call(
        lambda *refs: modes_kernel(1.0 / stack, planes, width, *refs),
        in_specs=[vmem, hbm],
        out_specs=[hbm, hbm],
        out_shape=[
            jax.ShapeDtypeStruct((planes * width, width), jnp.float32),
            jax.ShapeDtypeStruct((planes, rows_dev, width), jnp.float32),
        ],
        scratch_shapes=[
            pltpu.VMEM((planes * width, width), jnp.float32),
            pltpu.VMEM((width * planes, width), jnp.float32),
            pltpu.VMEM((width * planes, width), jnp.float32),
            pltpu.VMEM((planes, rows_dev, width), jnp.bfloat16),
            pltpu.VMEM((planes, rows_dev, width), jnp.float32),
            pltpu.SemaphoreType.DMA((planes,)),
            pltpu.SemaphoreType.DMA((planes * (rows_dev // TILE),)),
            pltpu.SemaphoreType.DMA,
        ],
        compiler_params=pltpu.CompilerParams(vmem_limit_bytes=LIMIT),
        name="factor_modes",
    )(packed, velocity)
    return (factor.reshape(planes, width, width), modes)


def solution(mesh):
    placed = (P(None, "rows", "batch"),)
    return jax.shard_map(
        shards,
        mesh=mesh,
        in_specs=placed,
        out_specs=(P(), P(None, "rows", "batch")),
        check_vma=False,
    )
```
